256 devices in a mesh: row: 32 (over x, y, core), col: 8 (over z).
Axes of the slice: x: 4, y: 4, z: 8, core: 2. Of those that a mesh axis runs over, the one named last changes fastest.
Arguments:
- panel: float32 [32768, 256], P(('row', 'col')), may hold values from -8 to 8
- diag_inverse: float32 [256, 256], replicated
- tiles: bfloat16 [10240, 256, 256], P(('row', 'col')), may hold values from -6 to 6
- tile_map: int32 [10240, 2], P(('row', 'col')), may hold values from -1 to 15, as said below
- send_list: int32 [1536], P(('row', 'col')), may hold values from -1 to 39, as said below
- place_list: int32 [8704], P(('row', 'col')), may hold values from -1 to 45, as said below
Outputs:
- factor_panel: float32 [32768, 256], P(('row', 'col'))
- balanced: bfloat16 [8704, 256, 256], P(('row', 'col'))
The draws below stay inside these ranges and needn't reach their ends.
Inputs may be any that keep to these rules, and one draw needn't show every extreme that they name: `tile_map`: each lower tile (I >= J) owned block-cyclically by a device appears in exactly one of its slots, in a drawn order; its other slots hold -1 in both entries. `send_list`: entries of a device name distinct live slots of that device, those it hands to its partner; unused entries are -1 and stand after the used ones. `place_list`: over a device's 34 entries, every live slot it does not hand over and every used send entry of its partner appear exactly once, in a drawn order; the rest are -1.
All inputs are finite; a program needn't handle non-finite values.
Results may differ from the reference program's by a relative error of at most 0.0051.
Values may be sent and summed in bfloat16 or wider, within the bound.
A program may use at most 128 MiB of HBM per device.

```python
import math
import jax
import jax.numpy as jnp
from jax import lax

TILE = 256
TILES = 128
ORDER = 32768
ROW_TILES = 4
COL_TILES = 16
SLOTS = 40
HELD = 34
MOVED = 6
N_ROW = 32
N_COL = 8
DEVICES = 256


def device_layout(key):
    base_key = jax.random.fold_in(key, 1009)
    cell_total = ROW_TILES * COL_TILES
    row_ids = jnp.arange(ROW_TILES, dtype=jnp.int32)[:, None]
    col_ids = jnp.arange(COL_TILES, dtype=jnp.int32)[None, :]
    slot_ids = jnp.arange(SLOTS, dtype=jnp.int32)

    def one_device(dev_key, rank_row, rank_col):
        key_cells, key_slots, key_live = jax.random.split(dev_key, 3)
        is_alive = (row_ids * N_ROW + rank_row >= col_ids * N_COL + rank_col).reshape(-1).astype(jnp.int32)
        scores = (1 - is_alive) * cell_total + jax.random.permutation(key_cells, cell_total).astype(jnp.int32)
        cell_ids = jnp.argsort(scores, stable=True)[:SLOTS].astype(jnp.int32)
        live_count = jnp.sum(is_alive)
        cell_ids = jnp.where(slot_ids < live_count, cell_ids, -1)
        cell_ids = jax.random.permutation(key_slots, cell_ids)
        tile_rows = jnp.where(cell_ids >= 0, cell_ids // COL_TILES, -1)
        tile_cols = jnp.where(cell_ids >= 0, cell_ids % COL_TILES, -1)
        slot_scores = jnp.where(cell_ids >= 0, jax.random.permutation(key_live, SLOTS).astype(jnp.int32), SLOTS + slot_ids)
        live_slots = jnp.argsort(slot_scores, stable=True).astype(jnp.int32)
        return (jnp.stack([tile_rows, tile_cols], 1), live_count, live_slots)
    dev_ids = jnp.arange(DEVICES, dtype=jnp.int32)
    rank_rows = dev_ids // N_COL
    rank_cols = dev_ids % N_COL
    dev_keys = jax.random.split(base_key, DEVICES)
    tile_maps, live_counts, live_slots = jax.vmap(one_device)(dev_keys, rank_rows, rank_cols)
    excess = jnp.maximum(live_counts - HELD, 0)
    partner = (N_ROW - 1 - rank_rows) * N_COL + rank_cols
    incoming = excess[partner]
    kept_count = live_counts - excess
    move_ids = jnp.arange(MOVED, dtype=jnp.int32)[None, :]
    picks = jnp.clip(kept_count[:, None] + move_ids, 0, SLOTS - 1)
    send_rows = jnp.where(move_ids < excess[:, None], jnp.take_along_axis(live_slots, picks, 1), -1)
    held_ids = jnp.arange(HELD, dtype=jnp.int32)[None, :]
    first_part = jnp.take_along_axis(live_slots, jnp.clip(held_ids, 0, SLOTS - 1), 1)
    later_part = jnp.where(held_ids < (kept_count + incoming)[:, None], SLOTS + held_ids - kept_count[:, None], -1)
    place_rows = jnp.where(held_ids < kept_count[:, None], first_part, later_part)
    place_keys = jax.random.split(jax.random.fold_in(base_key, 2), DEVICES)

    def mix_row(row_key, row_values):
        return jax.random.permutation(row_key, row_values)
    place_rows = jax.vmap(mix_row)(place_keys, place_rows)
    return (tile_maps.reshape(DEVICES * SLOTS, 2).astype(jnp.int32), send_rows.reshape(-1).astype(jnp.int32), place_rows.reshape(-1).astype(jnp.int32))


def draw_tile_map(key, part):
    return device_layout(key)[0]


def draw_send_list(key, part):
    return device_layout(key)[1]


def draw_place_list(key, part):
    return device_layout(key)[2]


def draw_diag_inverse(key, part):
    key_diag, key_off = jax.random.split(jax.random.fold_in(key, 3))
    row_ids = jnp.arange(TILE)[:, None]
    col_ids = jnp.arange(TILE)[None, :]
    diagonal = jax.random.uniform(key_diag, (TILE,), jnp.float32, 0.12, 0.25)
    lower_part = jax.random.normal(key_off, (TILE, TILE), jnp.float32) * (0.12 / math.sqrt(TILE))
    lower_part = jnp.where(row_ids > col_ids, lower_part, 0.0)
    return (lower_part + jnp.diag(diagonal)).astype(jnp.float32)


def block_scale(own_key, extent, cuts, least, high):
    loudness, own = 1.0, jax.random.fold_in(own_key, 6)
    for axis_at, parts in cuts:
        steps = jnp.exp(jax.random.uniform(jax.random.fold_in(own, axis_at), (parts,), jnp.float32, least / len(cuts), high / len(cuts)))
        loudness = loudness * jnp.repeat(steps, extent[axis_at] // parts).reshape([-1 if axis == axis_at else 1 for axis in range(len(extent))])
    return loudness


def normal_values(own_key, extent, spread, most, shards=(), kind=jnp.bfloat16):
    loudness = block_scale(own_key, extent, shards, -0.22, 0.18) if shards else 1.0
    values = jax.random.normal(own_key, extent, jnp.float32) * spread * loudness
    return jnp.minimum(jnp.maximum(values, -most), most).astype(kind)


def setup_inputs(seed: int = 0) -> dict:
    keys = jax.random.split(jax.random.key(seed), 7)
    panel = normal_values(keys[0], (ORDER, TILE), 1.5, 8.0, ((0, 256),), jnp.float32)
    diag_inverse = draw_diag_inverse(jax.random.fold_in(keys[6], 71), 0)
    tiles = normal_values(keys[2], (DEVICES * SLOTS, TILE, TILE), 1.0, 6.0, ((0, 256),))
    tile_map = draw_tile_map(jax.random.fold_in(keys[6], 71), 0)
    send_list = draw_send_list(jax.random.fold_in(keys[6], 71), 0)
    place_list = draw_place_list(jax.random.fold_in(keys[6], 71), 0)
    return {"panel": panel, "diag_inverse": diag_inverse, "tiles": tiles, "tile_map": tile_map, "send_list": send_list, "place_list": place_list}


def reference(panel, diag_inverse, tiles, tile_map, send_list, place_list):
    factor = jnp.dot(panel, diag_inverse.T, precision=lax.Precision.HIGHEST, preferred_element_type=jnp.float32)
    factor_tiles = factor.astype(jnp.bfloat16).reshape(TILES, TILE, TILE)
    send_rows = send_list.reshape(DEVICES, MOVED)
    place_rows = place_list.reshape(DEVICES, HELD)

    def one_device(device):
        rank_row = device // N_COL
        rank_col = device % N_COL
        partner = (N_ROW - 1 - rank_row) * N_COL + rank_col
        source = place_rows[device]
        remote = source >= SLOTS
        far_index = jnp.clip(source - SLOTS, 0, MOVED - 1)
        far_slot = send_rows[partner][far_index]
        owner = jnp.where(remote, partner, device)
        slot_index = jnp.clip(jnp.where(remote, far_slot, source), 0, SLOTS - 1)
        flat_index = (owner * SLOTS + slot_index).astype(jnp.int32)
        raw_tiles = tiles[flat_index]
        cell_rows = tile_map[flat_index]
        owner_row = owner // N_COL
        row_local = jnp.clip(cell_rows[:, 0], 0, ROW_TILES - 1)
        col_local = jnp.clip(cell_rows[:, 1], 0, COL_TILES - 1)
        left_tiles = factor_tiles[(owner_row * ROW_TILES + row_local).astype(jnp.int32)]
        col_global = col_local * N_COL + rank_col
        right_tiles = factor_tiles[((col_global % N_ROW) * ROW_TILES + col_global // N_ROW).astype(jnp.int32)]
        product = jnp.einsum("kil,kjl->kij", left_tiles.astype(jnp.float32), right_tiles.astype(jnp.float32))
        result = (raw_tiles.astype(jnp.float32) - product).astype(jnp.bfloat16)
        return jnp.where((source >= 0)[:, None, None], result, jnp.zeros((), jnp.bfloat16))

    balanced = lax.map(one_device, jnp.arange(DEVICES, dtype=jnp.int32))
    return factor, balanced.reshape(DEVICES * HELD, TILE, TILE)
```

```python
import functools

import jax
import jax.numpy as jnp
from jax import lax
from jax.experimental import pallas as pl
from jax.experimental.pallas import tpu as pltpu
from jax.sharding import PartitionSpec as P

MESH = pl.DeviceIdType.MESH
NX, NY, NZ = 4, 4, 8
GROUPS = ((0,), (1, -1), (2, -2), (3, -3), (4,))
PIECE = {0: 0, 1: 1, -1: 2, 2: 3, -2: 4, 3: 5, -3: 6, 4: 7}
PARTNER_TICK = 4


class Ids:
    def __init__(self):
        self.count = 0

    def take(self, n):
        first = self.count
        self.count += n
        return first


SEND, RECV = Ids(), Ids()
S_ZP, S_ZM, S_QP, S_QM = (SEND.take(4) for _ in range(4))
S_PP, S_INFO = SEND.take(1), SEND.take(1)
S_EX = SEND.take(6)
S_YI, S_YC, S_YO, S_XC, S_XI, S_XF = (SEND.take(8) for _ in range(6))
S_DD = SEND.take(32)
R_ZP, R_ZM, R_QP, R_QM = (RECV.take(4) for _ in range(4))
R_PP, R_INFO = RECV.take(1), RECV.take(1)
R_EX = RECV.take(6)
R_AY, R_RC, R_RI, R_RF = (RECV.take(8) for _ in range(4))
R_DD = RECV.take(32)


def solve(panel, inverse):
    return lax.dot_general(
        panel,
        inverse,
        (((1,), (1,)), ((), ())),
        precision=lax.Precision.HIGHEST,
        preferred_element_type=jnp.float32,
    )


def gather_kernel(
    panel_ref, inv_ref, tiles_ref, map_ref, send_ref,
    rows_ref, cols_ref, recv_ref, info_ref,
    tile_buf, send_buf, half, info_src, send_sem, recv_sem, local_sem,
):
    r = lax.axis_index("row")
    z = lax.axis_index("col")
    x, y, k = r // 8, (r // 2) % 4, r % 2

    def dev(px, py, pk, pz):
        return (px * 8 + py * 2 + pk, pz)

    xi, xc = x + 1 - 2 * (x % 2), 3 - x
    yi, yc = y + 1 - 2 * (y % 2), 3 - y
    d_zp, d_zm = dev(x, y, k, (z + 1) % NZ), dev(x, y, k, (z + NZ - 1) % NZ)
    d_part = dev(3 - x, 3 - y, 1 - k, z)
    d_xi, d_xc = dev(xi, y, k, z), dev(xc, y, k, z)
    d_yi, d_yc = dev(x, yi, k, z), dev(x, yc, k, z)
    d_core = dev(x, y, 1 - k, z)
    sy, sk = z // 2, z % 2

    barrier = pltpu.get_barrier_semaphore()
    friends = (d_zp, d_zm, d_part, d_xi, d_xc, d_yi, d_yc, d_core)
    for friend in friends:
        pl.semaphore_signal(barrier, inc=1, device_id=friend, device_id_type=MESH)

    load = pltpu.make_async_copy(tiles_ref, tile_buf, local_sem.at[0])
    load.start()
    half[...] = solve(panel_ref[...], inv_ref[...]).astype(jnp.bfloat16)
    keep = pltpu.make_async_copy(half, rows_ref.at[z], local_sem.at[1])
    keep.start()

    def copy(src, dst, s, t, device):
        return pltpu.make_async_remote_copy(
            src_ref=src, dst_ref=dst, send_sem=send_sem.at[s], recv_sem=recv_sem.at[t],
            device_id=device, device_id_type=MESH,
        )

    def zpos(off):
        return (z + off + NZ) % NZ

    def ring(base, h, up, s0, t0, own):
        at = base + zpos(-h if up else h)
        device = d_zp if up else d_zm
        if h < 3:
            src = own if h == 0 else rows_ref.at[at]
            return copy(src, rows_ref.at[at], s0 + h, t0 + h, device)
        part = pl.ds(0, 64) if up else pl.ds(64, 64)
        return copy(rows_ref.at[at, part], rows_ref.at[at, part], s0 + h, t0 + h, device)

    def ring_send(base, h, s_up, s_down, r_up, r_down, own):
        ring(base, h, True, s_up, r_up, own).start()
        ring(base, h, False, s_down, r_down, own).start()

    def ring_wait_send(base, h, s_up, s_down, r_up, r_down, own):
        ring(base, h, True, s_up, r_up, own).wait_send()
        ring(base, h, False, s_down, r_down, own).wait_send()

    def ring_wait_recv(base, h, r_up, r_down):
        if h < 4:
            for off, t in ((-h, r_up), (h, r_down)):
                at = rows_ref.at[base + zpos(off)]
                copy(at, at, 0, t + h - 1, d_zp).wait_recv()
        else:
            for part, t in ((pl.ds(0, 64), r_up), (pl.ds(64, 64), r_down)):
                at = rows_ref.at[base + zpos(4), part]
                copy(at, at, 0, t + 3, d_zp).wait_recv()

    own_args = (0, S_ZP, S_ZM, R_ZP, R_ZM, half)
    part_args = (8, S_QP, S_QM, R_QP, R_QM, rows_ref.at[8 + z])

    def own_send(h, go="start"):
        b, su, sd, ru, rd, own = own_args
        (ring_send if go == "start" else ring_wait_send)(b, h, su, sd, ru, rd, own)

    def part_send(h, go="start"):
        b, su, sd, ru, rd, own = part_args
        (ring_send if go == "start" else ring_wait_send)(b, h, su, sd, ru, rd, own)

    partner_piece = copy(half, rows_ref.at[8 + z], S_PP, R_PP, d_part)
    partner_info = copy(info_src, info_ref, S_INFO, R_INFO, d_part)
    exchange = [
        copy(send_buf.at[j], recv_ref.at[j], S_EX + j, R_EX + j, d_part) for j in range(6)
    ]

    def cols_at(block, off):
        return cols_ref.at[block * 8 + zpos(off)]

    def mine(off, source):
        if not source:
            return cols_at(x, off)
        return half if off == 0 else rows_ref.at[zpos(off)]

    def y_in(off, source):
        i = PIECE[off]
        return copy(mine(off, source), cols_at(x, off), S_YI + i, R_AY + i, d_yi)

    def y_cross(off, source):
        i = PIECE[off]
        return copy(mine(off, source), cols_at(x, off), S_YC + i, R_AY + i, d_yc)

    def y_over(off):
        i = PIECE[off]
        return copy(cols_at(x, off), cols_at(x, off), S_YO + i, R_AY + i, d_yi)

    def x_cross(off, source):
        i = PIECE[off]
        return copy(mine(off, source), cols_at(x, off), S_XC + i, R_RC + i, d_xc)

    def x_in(off, source):
        i = PIECE[off]
        return copy(mine(off, source), cols_at(x, off), S_XI + i, R_RI + i, d_xi)

    def x_forward(off):
        i = PIECE[off]
        return copy(cols_at(xc, off), cols_at(xc, off), S_XF + i, R_RF + i, d_xi)

    def to_core(which, off, source):
        block = (x, xc, xi, 3 - xi)[which]
        i = which * 8 + PIECE[off]
        src = mine(off, source) if which == 0 else cols_at(block, off)
        return copy(src, cols_at(block, off), S_DD + i, R_DD + i, d_core)

    def arrived(ref, t):
        copy(ref, ref, 0, t, d_core).wait_recv()

    pl.semaphore_wait(barrier, len(friends))
    own_send(0)
    partner_piece.start()

    def sequence(depth, plane):
        source = depth == 0
        for t in range(0, 9):
            if 1 <= t <= 4:
                ring_wait_recv(0, t, R_ZP, R_ZM)
                if t <= 3:
                    own_send(t)
            p = t - PARTNER_TICK
            if p == 0:
                partner_piece.wait_recv()
                part_send(0)
            elif 1 <= p <= 4:
                ring_wait_recv(8, p, R_QP, R_QM)
                if p <= 3:
                    part_send(p)
            if not plane:
                continue
            g = t - depth
            if 0 <= g <= 4:
                for off in GROUPS[g]:
                    if not source:
                        arrived(cols_at(x, off), R_AY + PIECE[off])
                    if source:
                        y_cross(off, source).start()
                        y_in(off, source).start()
                    if depth == 1:
                        @pl.when(y == 3 - sy)
                        def _():
                            y_over(off).start()
                    x_cross(off, source).start()
                    x_in(off, source).start()
                    to_core(0, off, source).start()
            g = t - depth - 1
            if 0 <= g <= 4:
                for off in GROUPS[g]:
                    arrived(cols_at(xc, off), R_RC + PIECE[off])
                    x_forward(off).start()
                    to_core(1, off, source).start()
                for off in GROUPS[g]:
                    arrived(cols_at(xi, off), R_RI + PIECE[off])
                    to_core(2, off, source).start()
            g = t - depth - 2
            if 0 <= g <= 4:
                for off in GROUPS[g]:
                    arrived(cols_at(3 - xi, off), R_RF + PIECE[off])
                    to_core(3, off, source).start()
        if source:
            fill = pltpu.make_async_copy(
                rows_ref.at[pl.ds(0, 8)], cols_ref.at[pl.ds(x * 8, 8)], local_sem.at[2]
            )
            keep.wait()
            fill.start()
            fill.wait()
        if plane:
            for off in PIECE:
                if source:
                    y_in(off, source).wait_send()
                    y_cross(off, source).wait_send()
                if depth == 1:
                    @pl.when(y == 3 - sy)
                    def _():
                        y_over(off).wait_send()
                x_cross(off, source).wait_send()
                x_in(off, source).wait_send()
                x_forward(off).wait_send()
                for which in range(4):
                    to_core(which, off, source).wait_send()
        else:
            for which in range(4):
                block = (x, xc, xi, 3 - xi)[which]
                for off in PIECE:
                    arrived(cols_at(block, off), R_DD + which * 8 + PIECE[off])
        if not source:
            keep.wait()

    load.wait()
    lane = lax.broadcasted_iota(jnp.int32, (8, 128), 1)
    sub = lax.broadcasted_iota(jnp.int32, (8, 128), 0)
    info = jnp.zeros((8, 128), jnp.int32)
    for j in range(6):
        slot = jnp.clip(send_ref[j], 0, 39)
        send_buf[j] = tile_buf[slot]
        info = jnp.where((sub == j) & (lane == 0), map_ref[slot, 0], info)
        info = jnp.where((sub == j) & (lane == 1), map_ref[slot, 1], info)
    info_src[...] = info
    partner_info.start()
    for item in exchange:
        item.start()

    on_plane = k == sk
    is_source = y == sy
    is_far = y == (3 - sy) + 1 - 2 * ((3 - sy) % 2)

    @pl.when(on_plane & is_source)
    def _():
        sequence(0, True)

    @pl.when(on_plane & jnp.logical_not(is_source) & jnp.logical_not(is_far))
    def _():
        sequence(1, True)

    @pl.when(on_plane & is_far)
    def _():
        sequence(2, True)

    @pl.when(jnp.logical_not(on_plane))
    def _():
        sequence(9, False)

    for h in range(4):
        own_send(h, "wait")
        part_send(h, "wait")
    partner_piece.wait_send()
    partner_info.wait()
    for item in exchange:
        item.wait()


def update_kernel(
    place_ref, map_ref, info_ref, panel_ref, inv_ref, tiles_ref, rows_ref, cols_ref, recv_ref,
    factor_ref, out_ref, raw, left, right, in_sem, out_sem, fac_sem,
):
    held = out_ref.shape[0]
    load_left = pltpu.make_async_copy(rows_ref, left, fac_sem.at[0])
    load_right = pltpu.make_async_copy(cols_ref, right, fac_sem.at[1])
    load_left.start()
    load_right.start()

    def fetch(j):
        s = place_ref[j]

        @pl.when((s >= 0) & (s < 40))
        def _():
            pltpu.make_async_copy(
                tiles_ref.at[jnp.clip(s, 0, 39)], raw.at[j], in_sem.at[j]
            ).start()

        @pl.when(s >= 40)
        def _():
            pltpu.make_async_copy(
                recv_ref.at[jnp.clip(s - 40, 0, 5)], raw.at[j], in_sem.at[j]
            ).start()

    pl.loop(0, held)(fetch)
    factor_ref[...] = solve(panel_ref[...], inv_ref[...])
    load_left.wait()
    load_right.wait()

    def renew(j):
        s = place_ref[j]
        far = s >= 40
        near_slot = jnp.clip(s, 0, 39)
        far_slot = jnp.clip(s - 40, 0, 5)
        a = jnp.where(far, info_ref[far_slot, 0], map_ref[near_slot, 0])
        b = jnp.where(far, info_ref[far_slot, 1], map_ref[near_slot, 1])
        a = jnp.clip(a, 0, 3)
        b = jnp.clip(b, 0, 15)

        @pl.when(s >= 0)
        def _():
            pltpu.make_async_copy(tiles_ref.at[0], raw.at[j], in_sem.at[j]).wait()
            product = lax.dot_general(
                left[jnp.where(far, 4, 0) + a],
                right[(b % 4) * 4 + b // 4],
                (((1,), (1,)), ((), ())),
                preferred_element_type=jnp.float32,
            )
            raw[j] = (raw[j].astype(jnp.float32) - product).astype(jnp.bfloat16)

        @pl.when(s < 0)
        def _():
            raw[j] = jnp.zeros((256, 256), jnp.bfloat16)

        pltpu.make_async_copy(raw.at[j], out_ref.at[j], out_sem.at[j]).start()

    pl.loop(0, held)(renew)

    def finish(j):
        pltpu.make_async_copy(raw.at[j], out_ref.at[j], out_sem.at[j]).wait()

    pl.loop(0, held)(finish)


def shards(panel, diag_inverse, tiles, tile_map, send_list, place_list):
    vmem = pl.BlockSpec(memory_space=pltpu.VMEM)
    smem = pl.BlockSpec(memory_space=pltpu.SMEM)
    anyw = pl.BlockSpec(memory_space=pl.ANY)
    bf16 = jnp.bfloat16
    held = place_list.shape[0]
    rows, cols, recv, info = pl.pallas_call(
        gather_kernel,
        out_shape=(
            jax.ShapeDtypeStruct((16, 128, 256), bf16),
            jax.ShapeDtypeStruct((32, 128, 256), bf16),
            jax.ShapeDtypeStruct((6, 256, 256), bf16),
            jax.ShapeDtypeStruct((8, 128), jnp.int32),
        ),
        in_specs=[vmem, vmem, anyw, smem, smem],
        out_specs=(anyw, anyw, anyw, anyw),
        scratch_shapes=[
            pltpu.VMEM((40, 256, 256), bf16),
            pltpu.VMEM((6, 256, 256), bf16),
            pltpu.VMEM((128, 256), bf16),
            pltpu.VMEM((8, 128), jnp.int32),
            pltpu.SemaphoreType.DMA((SEND.count,)),
            pltpu.SemaphoreType.DMA((RECV.count,)),
            pltpu.SemaphoreType.DMA((3,)),
        ],
        compiler_params=pltpu.CompilerParams(
            collective_id=0, has_side_effects=True, vmem_limit_bytes=24 * 1024 * 1024
        ),
        name="gather_and_exchange",
    )(panel, diag_inverse, tiles, tile_map, send_list)
    left = rows.reshape(8, 256, 256)
    right = cols.reshape(16, 256, 256)
    return pl.pallas_call(
        update_kernel,
        out_shape=(
            jax.ShapeDtypeStruct((128, 256), jnp.float32),
            jax.ShapeDtypeStruct((held, 256, 256), bf16),
        ),
        in_specs=[smem, smem, smem, vmem, vmem, anyw, anyw, anyw, anyw],
        out_specs=(vmem, anyw),
        scratch_shapes=[
            pltpu.VMEM((held, 256, 256), bf16),
            pltpu.VMEM((8, 256, 256), bf16),
            pltpu.VMEM((16, 256, 256), bf16),
            pltpu.SemaphoreType.DMA((held,)),
            pltpu.SemaphoreType.DMA((held,)),
            pltpu.SemaphoreType.DMA((2,)),
        ],
        compiler_params=pltpu.CompilerParams(vmem_limit_bytes=24 * 1024 * 1024),
        name="update_and_place",
    )(place_list, tile_map, info, panel, diag_inverse, tiles, left, right, recv)


def solution(mesh):
    in_specs = (
        P(("row", "col"), None),
        P(),
        P(("row", "col"), None, None),
        P(("row", "col"), None),
        P(("row", "col")),
        P(("row", "col")),
    )
    out_specs = (P(("row", "col"), None), P(("row", "col"), None, None))
    return jax.shard_map(shards, mesh=mesh, in_specs=in_specs, out_specs=out_specs, check_vma=False)
```

```python
import functools

import jax
import jax.numpy as jnp
from jax import lax
from jax.experimental import pallas as pl
from jax.experimental.pallas import tpu as pltpu
from jax.sharding import PartitionSpec as P

MESH = pl.DeviceIdType.MESH
NX, NY, NZ = 4, 4, 8
PLACE = {0: 0, 1: 1, -1: 2, 2: 3, -2: 4, 3: 5, -3: 6, 4: 7, -4: 7}
HOPS = ((0, 1), (1, 2), (3, 2), (5, 2), (7, 1))
PARTS = ((0, 5, 2), (5, 3, 4))
PARTNER_TICK = 2
EXCHANGE_TICK = (0, 1, 2, 4, 6, 8)


class Ids:
    def __init__(self):
        self.count = 0

    def take(self, n):
        first = self.count
        self.count += n
        return first


SEND, RECV = Ids(), Ids()
S_ZP, S_ZM, S_QP, S_QM = (SEND.take(4) for _ in range(4))
S_PP, S_INFO = SEND.take(1), SEND.take(1)
S_EX = SEND.take(6)
S_YI, S_YC, S_YO, S_XC, S_XI, S_XF = (SEND.take(5) for _ in range(6))
S_DD = SEND.take(8)
R_ZP, R_ZM, R_QP, R_QM = (RECV.take(4) for _ in range(4))
R_PP, R_INFO = RECV.take(1), RECV.take(1)
R_EX = RECV.take(6)
R_AY, R_RC, R_RI, R_RF = (RECV.take(5) for _ in range(4))
R_DD = RECV.take(8)


def solve(panel, inverse):
    return lax.dot_general(
        panel,
        inverse,
        (((1,), (1,)), ((), ())),
        precision=lax.Precision.HIGHEST,
        preferred_element_type=jnp.float32,
    )


def product(left, right):
    return lax.dot_general(
        left, right, (((1,), (1,)), ((), ())), preferred_element_type=jnp.float32
    )


def panel_kernel(
    panel_hbm, inv_hbm, tiles_hbm, map_hbm, send_hbm,
    factor_ref, pool,
    panel_ref, inv_ref, map_ref, send_ref, rows_ref, cols_ref,
    send_buf, recv_buf, info_src, info_ref, info_at, send_sem, recv_sem, local_sem,
):
    r = lax.axis_index("row")
    z = lax.axis_index("col")
    x, y, k = r // 8, (r // 2) % 4, r % 2

    def dev(px, py, pk, pz):
        return (px * 8 + py * 2 + pk, pz)

    xi, xc = x + 1 - 2 * (x % 2), 3 - x
    yi, yc = y + 1 - 2 * (y % 2), 3 - y
    d_zp, d_zm = dev(x, y, k, (z + 1) % NZ), dev(x, y, k, (z + NZ - 1) % NZ)
    d_part = dev(3 - x, 3 - y, 1 - k, z)
    d_xi, d_xc = dev(xi, y, k, z), dev(xc, y, k, z)
    d_yi, d_yc = dev(x, yi, k, z), dev(x, yc, k, z)
    d_core = dev(x, y, 1 - k, z)
    sy, sk = z // 2, z % 2

    barrier = pltpu.get_barrier_semaphore()
    friends = (d_zp, d_zm, d_part, d_xi, d_xc, d_yi, d_yc, d_core)
    for friend in friends:
        pl.semaphore_signal(barrier, inc=1, device_id=friend, device_id_type=MESH)

    def local(src, dst, i):
        return pltpu.make_async_copy(src, dst, local_sem.at[i])

    load_panel = local(panel_hbm, panel_ref, 0)
    load_inv = local(inv_hbm, inv_ref, 1)
    load_map = local(map_hbm, map_ref, 2)
    load_send = local(send_hbm, send_ref, 3)
    load_tiles = local(tiles_hbm, pool.at[pl.ds(0, 40)], 4)
    for item in (load_panel, load_inv, load_map, load_send, load_tiles):
        item.start()
    load_panel.wait()
    load_inv.wait()
    factor = solve(panel_ref[...], inv_ref[...])
    factor_ref[...] = factor
    rows_ref[0] = factor.astype(jnp.bfloat16)

    def copy(src, dst, s, t, device):
        return pltpu.make_async_remote_copy(
            src_ref=src, dst_ref=dst, send_sem=send_sem.at[s], recv_sem=recv_sem.at[t],
            device_id=device, device_id_type=MESH,
        )

    def ring(base, h, up, s0, t0):
        sign = -1 if up else 1
        src, dst = base + PLACE[sign * h], base + PLACE[sign * (h + 1)]
        device = d_zp if up else d_zm
        if h < 3:
            return copy(rows_ref.at[src], rows_ref.at[dst], s0 + h, t0 + h, device)
        part = pl.ds(0, 64) if up else pl.ds(64, 64)
        return copy(rows_ref.at[src, part], rows_ref.at[dst, part], s0 + h, t0 + h, device)

    def ring_wait_recv(base, h, r_up, r_down):
        for sign, t, part in ((-1, r_up, pl.ds(0, 64)), (1, r_down, pl.ds(64, 64))):
            at = rows_ref.at[base + PLACE[sign * h]]
            if h == 4:
                at = rows_ref.at[base + PLACE[4], part]
            copy(at, at, 0, t + h - 1, d_zp).wait_recv()

    def own_hop(h):
        return (ring(0, h, True, S_ZP, R_ZP), ring(0, h, False, S_ZM, R_ZM))

    def part_hop(h):
        return (ring(8, h, True, S_QP, R_QP), ring(8, h, False, S_QM, R_QM))

    def start(copies):
        for item in copies:
            item.start()

    partner_piece = copy(rows_ref.at[0], rows_ref.at[8], S_PP, R_PP, d_part)
    partner_info = copy(info_src, info_ref, S_INFO, R_INFO, d_part)
    exchange = [
        copy(send_buf.at[j], recv_buf.at[j], S_EX + j, R_EX + j, d_part) for j in range(6)
    ]

    def cols_at(block, g):
        return cols_ref.at[pl.ds(block * 8 + HOPS[g][0], HOPS[g][1])]

    def mine(g, source):
        return rows_ref.at[pl.ds(*HOPS[g])] if source else cols_at(x, g)

    def y_in(g, source):
        return copy(mine(g, source), cols_at(x, g), S_YI + g, R_AY + g, d_yi)

    def y_cross(g, source):
        return copy(mine(g, source), cols_at(x, g), S_YC + g, R_AY + g, d_yc)

    def y_over(g):
        return copy(cols_at(x, g), cols_at(x, g), S_YO + g, R_AY + g, d_yi)

    def x_cross(g, source):
        return copy(mine(g, source), cols_at(x, g), S_XC + g, R_RC + g, d_xc)

    def x_in(g, source):
        return copy(mine(g, source), cols_at(x, g), S_XI + g, R_RI + g, d_xi)

    def x_forward(g):
        return copy(cols_at(xc, g), cols_at(xc, g), S_XF + g, R_RF + g, d_xi)

    def to_core(which, p, source):
        block = (x, xc, xi, 3 - xi)[which]
        first, count, _ = PARTS[p]
        dst = cols_ref.at[pl.ds(block * 8 + first, count)]
        src = rows_ref.at[pl.ds(first, count)] if source and which == 0 else dst
        return copy(src, dst, S_DD + which * 2 + p, R_DD + which * 2 + p, d_core)

    def pass_on(which, g, source):
        for p in range(2):
            if PARTS[p][2] == g:
                to_core(which, p, source).start()

    def arrived(ref, t):
        copy(ref, ref, 0, t, d_core).wait_recv()

    pl.semaphore_wait(barrier, len(friends))
    start(own_hop(0))
    partner_piece.start()
    load_map.wait()
    load_send.wait()
    load_tiles.wait()
    lane = lax.broadcasted_iota(jnp.int32, (8, 128), 1)
    sub = lax.broadcasted_iota(jnp.int32, (8, 128), 0)
    info = jnp.zeros((8, 128), jnp.int32)
    for j in range(6):
        slot = jnp.clip(send_ref[j], 0, 39)
        send_buf[j] = pool[slot]
        info = jnp.where((sub == j) & (lane == 0), map_ref[0, slot], info)
        info = jnp.where((sub == j) & (lane == 1), map_ref[1, slot], info)
    info_src[...] = info
    partner_info.start()


    def sequence(depth, plane):
        source = depth == 0
        for t in range(0, 9):
            for j in range(6):
                if EXCHANGE_TICK[j] == t:
                    exchange[j].start()
            if 1 <= t <= 4:
                ring_wait_recv(0, t, R_ZP, R_ZM)
                if t <= 3:
                    start(own_hop(t))
            p = t - PARTNER_TICK
            if p == 0:
                partner_piece.wait_recv()
                start(part_hop(0))
            elif 1 <= p <= 4:
                ring_wait_recv(8, p, R_QP, R_QM)
                if p <= 3:
                    start(part_hop(p))
            if not plane:
                continue
            g = t - depth
            if 0 <= g <= 4:
                if source:
                    y_cross(g, source).start()
                    y_in(g, source).start()
                else:
                    arrived(cols_at(x, g), R_AY + g)
                if depth == 1:
                    @pl.when(y == 3 - sy)
                    def _():
                        y_over(g).start()
                x_cross(g, source).start()
                x_in(g, source).start()
                pass_on(0, g, source)
            g = t - depth - 1
            if 0 <= g <= 4:
                arrived(cols_at(xc, g), R_RC + g)
                x_forward(g).start()
                pass_on(1, g, source)
                arrived(cols_at(xi, g), R_RI + g)
                pass_on(2, g, source)
            g = t - depth - 2
            if 0 <= g <= 4:
                arrived(cols_at(3 - xi, g), R_RF + g)
                pass_on(3, g, source)
        if source:
            for i in range(8):
                cols_ref[x * 8 + i] = rows_ref[i]
        if plane:
            for g in range(5):
                if source:
                    y_in(g, source).wait_send()
                    y_cross(g, source).wait_send()
                if depth == 1:
                    @pl.when(y == 3 - sy)
                    def _():
                        y_over(g).wait_send()
                x_cross(g, source).wait_send()
                x_in(g, source).wait_send()
                x_forward(g).wait_send()
            for which in range(4):
                for p in range(2):
                    to_core(which, p, source).wait_send()
        else:
            for which in range(4):
                for p in range(2):
                    to_core(which, p, False).wait_recv()

    on_plane = k == sk
    is_source = y == sy
    is_far = y == (3 - sy) + 1 - 2 * ((3 - sy) % 2)

    @pl.when(on_plane & is_source)
    def _():
        sequence(0, True)

    @pl.when(on_plane & jnp.logical_not(is_source) & jnp.logical_not(is_far))
    def _():
        sequence(1, True)

    @pl.when(on_plane & is_far)
    def _():
        sequence(2, True)

    @pl.when(jnp.logical_not(on_plane))
    def _():
        sequence(9, False)


    def both_halves(ref, base, tile):
        def half(at):
            off = lax.rem(at - z + NZ, NZ)
            return ref[base + jnp.where(off <= 4, jnp.maximum(2 * off - 1, 0), 2 * (NZ - off))]

        return jnp.concatenate([half(2 * tile), half(2 * tile + 1)], 0)

    def factors(a, b, far):
        a = jnp.clip(a, 0, 3)
        b = jnp.clip(b, 0, 15)
        return product(both_halves(rows_ref, 8 * far, a), both_halves(cols_ref, (b % 4) * 8, b // 4))

    def renew(raw, first, count, parts):
        for u in range(count):
            value = raw(u).astype(jnp.float32) - parts[u]
            pool[first + u] = value.astype(jnp.bfloat16)

    @pl.loop(0, 5)
    def _(q):
        parts = [factors(map_ref[0, q * 8 + u], map_ref[1, q * 8 + u], 0) for u in range(8)]
        renew(lambda u: pool[q * 8 + u], q * 8, 8, parts)

    partner_info.wait()
    place_info = local(info_ref, info_at, 2)
    place_info.start()
    place_info.wait()
    for item in exchange:
        item.wait()
    parts = [factors(info_at[u, 0], info_at[u, 1], 1) for u in range(6)]
    renew(lambda u: recv_buf[u], 40, 6, parts)
    for h in range(4):
        for item in own_hop(h) + part_hop(h):
            item.wait_send()
    partner_piece.wait_send()


def place_kernel(place_ref, pool_ref, factor_in, factor_out, out_ref, zeros, sem, factor_sem):
    held = out_ref.shape[0]
    factor_copy = pltpu.make_async_copy(factor_in, factor_out, factor_sem)
    factor_copy.start()
    zeros[...] = jnp.zeros_like(zeros)

    @pl.loop(0, held)
    def _(j):
        s = place_ref[j]

        @pl.when(s >= 0)
        def _():
            pltpu.make_async_copy(pool_ref.at[jnp.clip(s, 0, 45)], out_ref.at[j], sem.at[j]).start()

        @pl.when(s < 0)
        def _():
            pltpu.make_async_copy(zeros, out_ref.at[j], sem.at[j]).start()

    @pl.loop(0, held)
    def _(j):
        pltpu.make_async_copy(zeros, out_ref.at[j], sem.at[j]).wait()

    factor_copy.wait()


def shards(panel, diag_inverse, tiles, tile_map, send_list, place_list):
    vmem = pl.BlockSpec(memory_space=pltpu.VMEM)
    smem = pl.BlockSpec(memory_space=pltpu.SMEM)
    hbm = pl.BlockSpec(memory_space=pltpu.HBM)
    bf16 = jnp.bfloat16
    held = place_list.shape[0]
    factor, pool = pl.pallas_call(
        panel_kernel,
        out_shape=(
            pltpu.VMEM((128, 256), jnp.float32),
            pltpu.VMEM((46, 256, 256), bf16),
        ),
        in_specs=[hbm] * 5,
        out_specs=(vmem, vmem),
        scratch_shapes=[
            pltpu.VMEM((128, 256), jnp.float32),
            pltpu.VMEM((256, 256), jnp.float32),
            pltpu.SMEM((2, 40), jnp.int32),
            pltpu.SMEM((6,), jnp.int32),
            pltpu.VMEM((16, 128, 256), bf16),
            pltpu.VMEM((32, 128, 256), bf16),
            pltpu.VMEM((6, 256, 256), bf16),
            pltpu.VMEM((6, 256, 256), bf16),
            pltpu.VMEM((8, 128), jnp.int32),
            pltpu.VMEM((8, 128), jnp.int32),
            pltpu.SMEM((8, 128), jnp.int32),
            pltpu.SemaphoreType.DMA((SEND.count,)),
            pltpu.SemaphoreType.DMA((RECV.count,)),
            pltpu.SemaphoreType.DMA((5,)),
        ],
        compiler_params=pltpu.CompilerParams(
            collective_id=0, has_side_effects=True, vmem_limit_bytes=54 * 1024 * 1024
        ),
        name="gather_exchange_renew",
    )(panel, diag_inverse, tiles, tile_map.T, send_list)
    return pl.pallas_call(
        place_kernel,
        out_shape=(
            jax.ShapeDtypeStruct((128, 256), jnp.float32),
            jax.ShapeDtypeStruct((held, 256, 256), bf16),
        ),
        in_specs=[smem, pl.BlockSpec(memory_space=pl.ANY), pl.BlockSpec(memory_space=pl.ANY)],
        out_specs=(hbm, hbm),
        scratch_shapes=[
            pltpu.VMEM((256, 256), bf16),
            pltpu.SemaphoreType.DMA((held,)),
            pltpu.SemaphoreType.DMA,
        ],
        compiler_params=pltpu.CompilerParams(vmem_limit_bytes=4 * 1024 * 1024),
        name="place",
    )(place_list, pool, factor)


def solution(mesh):
    in_specs = (
        P(("row", "col"), None),
        P(),
        P(("row", "col"), None, None),
        P(("row", "col"), None),
        P(("row", "col")),
        P(("row", "col")),
    )
    out_specs = (P(("row", "col"), None), P(("row", "col"), None, None))
    return jax.shard_map(shards, mesh=mesh, in_specs=in_specs, out_specs=out_specs, check_vma=False)
```

```python
import functools

import jax
import jax.numpy as jnp
from jax import lax
from jax.experimental import pallas as pl
from jax.experimental.pallas import tpu as pltpu
from jax.sharding import PartitionSpec as P

MESH = pl.DeviceIdType.MESH
NX, NY, NZ = 4, 4, 8
PLACE = {0: 0, 1: 1, -1: 2, 2: 3, -2: 4, 3: 5, -3: 6, 4: 7, -4: 7}
HOPS = ((0, 1), (1, 2), (3, 2), (5, 2), (7, 1))
PARTS = ((0, 5, 2), (5, 3, 4))
PARTNER_TICK = 2
EXCHANGE_TICK = (0, 1, 2, 4, 6, 8)


class Ids:
    def __init__(self):
        self.count = 0

    def take(self, n):
        first = self.count
        self.count += n
        return first


SEND, RECV = Ids(), Ids()
S_ZP, S_ZM, S_QP, S_QM = (SEND.take(4) for _ in range(4))
S_PP, S_INFO = SEND.take(1), SEND.take(1)
S_EX = SEND.take(6)
S_YI, S_YC, S_YO, S_XC, S_XI, S_XF = (SEND.take(5) for _ in range(6))
S_DD = SEND.take(8)
R_ZP, R_ZM, R_QP, R_QM = (RECV.take(4) for _ in range(4))
R_PP, R_INFO = RECV.take(1), RECV.take(1)
R_EX = RECV.take(6)
R_AY, R_RC, R_RI, R_RF = (RECV.take(5) for _ in range(4))
R_DD = RECV.take(8)


def solve(panel, inverse):
    return lax.dot_general(
        panel,
        inverse,
        (((1,), (1,)), ((), ())),
        precision=lax.Precision.HIGHEST,
        preferred_element_type=jnp.float32,
    )


def product(left, right):
    return lax.dot_general(
        left, right, (((1,), (1,)), ((), ())), preferred_element_type=jnp.float32
    )


def panel_kernel(
    panel_hbm, inv_hbm, tiles_hbm, map_hbm, send_hbm,
    factor_ref, pool,
    panel_ref, inv_ref, map_ref, send_ref, rows_ref, cols_ref,
    send_buf, recv_buf, info_src, info_ref, info_at, send_sem, recv_sem, local_sem,
):
    r = lax.axis_index("row")
    z = lax.axis_index("col")
    x, y, k = r // 8, (r // 2) % 4, r % 2

    def dev(px, py, pk, pz):
        return (px * 8 + py * 2 + pk, pz)

    xi, xc = x + 1 - 2 * (x % 2), 3 - x
    yi, yc = y + 1 - 2 * (y % 2), 3 - y
    d_zp, d_zm = dev(x, y, k, (z + 1) % NZ), dev(x, y, k, (z + NZ - 1) % NZ)
    d_part = dev(3 - x, 3 - y, 1 - k, z)
    d_xi, d_xc = dev(xi, y, k, z), dev(xc, y, k, z)
    d_yi, d_yc = dev(x, yi, k, z), dev(x, yc, k, z)
    d_core = dev(x, y, 1 - k, z)
    d_far = dev(x, 3 - yi, k, z)
    sy, sk = z // 2, z % 2

    barrier = pltpu.get_barrier_semaphore()
    friends = (d_zp, d_zm, d_part, d_xi, d_xc, d_yi, d_yc, d_far, d_core)
    for friend in friends:
        pl.semaphore_signal(barrier, inc=1, device_id=friend, device_id_type=MESH)

    def local(src, dst, i):
        return pltpu.make_async_copy(src, dst, local_sem.at[i])

    load_panel = local(panel_hbm, panel_ref, 0)
    load_inv = local(inv_hbm, inv_ref, 1)
    load_map = local(map_hbm, map_ref, 2)
    load_send = local(send_hbm, send_ref, 3)
    load_tiles = local(tiles_hbm, pool.at[pl.ds(0, 40)], 4)
    for item in (load_panel, load_inv, load_map, load_send, load_tiles):
        item.start()
    load_panel.wait()
    load_inv.wait()
    factor = solve(panel_ref[...], inv_ref[...])
    factor_ref[...] = factor
    rows_ref[0] = factor.astype(jnp.bfloat16)

    def copy(src, dst, s, t, device):
        return pltpu.make_async_remote_copy(
            src_ref=src, dst_ref=dst, send_sem=send_sem.at[s], recv_sem=recv_sem.at[t],
            device_id=device, device_id_type=MESH,
        )

    def ring(base, h, up, s0, t0):
        sign = -1 if up else 1
        src, dst = base + PLACE[sign * h], base + PLACE[sign * (h + 1)]
        device = d_zp if up else d_zm
        if h < 3:
            return copy(rows_ref.at[src], rows_ref.at[dst], s0 + h, t0 + h, device)
        part = pl.ds(0, 64) if up else pl.ds(64, 64)
        return copy(rows_ref.at[src, part], rows_ref.at[dst, part], s0 + h, t0 + h, device)

    def ring_wait_recv(base, h, r_up, r_down):
        for sign, t, part in ((-1, r_up, pl.ds(0, 64)), (1, r_down, pl.ds(64, 64))):
            at = rows_ref.at[base + PLACE[sign * h]]
            if h == 4:
                at = rows_ref.at[base + PLACE[4], part]
            copy(at, at, 0, t + h - 1, d_zp).wait_recv()

    def own_hop(h):
        return (ring(0, h, True, S_ZP, R_ZP), ring(0, h, False, S_ZM, R_ZM))

    def part_hop(h):
        return (ring(8, h, True, S_QP, R_QP), ring(8, h, False, S_QM, R_QM))

    def start(copies):
        for item in copies:
            item.start()

    partner_piece = copy(rows_ref.at[0], rows_ref.at[8], S_PP, R_PP, d_part)
    partner_info = copy(info_src, info_ref, S_INFO, R_INFO, d_part)
    exchange = [
        copy(send_buf.at[j], recv_buf.at[j], S_EX + j, R_EX + j, d_part) for j in range(6)
    ]

    def cols_at(block, g):
        return cols_ref.at[pl.ds(block * 8 + HOPS[g][0], HOPS[g][1])]

    def mine(g, source):
        return rows_ref.at[pl.ds(*HOPS[g])] if source else cols_at(x, g)

    def y_in(g, source):
        return copy(mine(g, source), cols_at(x, g), S_YI + g, R_AY + g, d_yi)

    def y_cross(g, source):
        return copy(mine(g, source), cols_at(x, g), S_YC + g, R_AY + g, d_yc)

    def y_over(g):
        return copy(mine(g, True), cols_at(x, g), S_YO + g, R_AY + g, d_far)

    def x_cross(g, source):
        return copy(mine(g, source), cols_at(x, g), S_XC + g, R_RC + g, d_xc)

    def x_in(g, source):
        return copy(mine(g, source), cols_at(x, g), S_XI + g, R_RI + g, d_xi)

    def x_forward(g):
        return copy(cols_at(xc, g), cols_at(xc, g), S_XF + g, R_RF + g, d_xi)

    def to_core(which, p, source):
        block = (x, xc, xi, 3 - xi)[which]
        first, count, _ = PARTS[p]
        dst = cols_ref.at[pl.ds(block * 8 + first, count)]
        src = rows_ref.at[pl.ds(first, count)] if source and which == 0 else dst
        return copy(src, dst, S_DD + which * 2 + p, R_DD + which * 2 + p, d_core)

    def pass_on(which, g, source):
        for p in range(2):
            if PARTS[p][2] == g:
                to_core(which, p, source).start()

    def arrived(ref, t):
        copy(ref, ref, 0, t, d_core).wait_recv()

    pl.semaphore_wait(barrier, len(friends))
    start(own_hop(0))
    partner_piece.start()
    load_map.wait()
    load_send.wait()
    load_tiles.wait()
    lane = lax.broadcasted_iota(jnp.int32, (8, 128), 1)
    sub = lax.broadcasted_iota(jnp.int32, (8, 128), 0)
    info = jnp.zeros((8, 128), jnp.int32)
    for j in range(6):
        slot = jnp.clip(send_ref[j], 0, 39)
        send_buf[j] = pool[slot]
        info = jnp.where((sub == j) & (lane == 0), map_ref[0, slot], info)
        info = jnp.where((sub == j) & (lane == 1), map_ref[1, slot], info)
    info_src[...] = info
    partner_info.start()


    def sequence(depth, plane):
        source = depth == 0
        for t in range(0, 9):
            for j in range(6):
                if EXCHANGE_TICK[j] == t:
                    exchange[j].start()
            if 1 <= t <= 4:
                ring_wait_recv(0, t, R_ZP, R_ZM)
                if t <= 3:
                    start(own_hop(t))
            p = t - PARTNER_TICK
            if p == 0:
                partner_piece.wait_recv()
                start(part_hop(0))
            elif 1 <= p <= 4:
                ring_wait_recv(8, p, R_QP, R_QM)
                if p <= 3:
                    start(part_hop(p))
            if not plane:
                continue
            g = t - depth
            if 0 <= g <= 4:
                if source:
                    y_cross(g, source).start()
                    y_over(g).start()
                    y_in(g, source).start()
                else:
                    arrived(cols_at(x, g), R_AY + g)
                x_cross(g, source).start()
                x_in(g, source).start()
                pass_on(0, g, source)
            g = t - depth - 1
            if 0 <= g <= 4:
                arrived(cols_at(xc, g), R_RC + g)
                x_forward(g).start()
                pass_on(1, g, source)
                arrived(cols_at(xi, g), R_RI + g)
                pass_on(2, g, source)
            g = t - depth - 2
            if 0 <= g <= 4:
                arrived(cols_at(3 - xi, g), R_RF + g)
                pass_on(3, g, source)
        if source:
            for i in range(8):
                cols_ref[x * 8 + i] = rows_ref[i]
        if plane:
            for g in range(5):
                if source:
                    y_in(g, source).wait_send()
                    y_over(g).wait_send()
                    y_cross(g, source).wait_send()
                x_cross(g, source).wait_send()
                x_in(g, source).wait_send()
                x_forward(g).wait_send()
            for which in range(4):
                for p in range(2):
                    to_core(which, p, source).wait_send()
        else:
            for which in range(4):
                for p in range(2):
                    to_core(which, p, False).wait_recv()

    on_plane = k == sk
    is_source = y == sy
    is_far = y == (3 - sy) + 1 - 2 * ((3 - sy) % 2)

    @pl.when(on_plane & is_source)
    def _():
        sequence(0, True)

    @pl.when(on_plane & jnp.logical_not(is_source) & jnp.logical_not(is_far))
    def _():
        sequence(1, True)

    @pl.when(on_plane & is_far)
    def _():
        sequence(1, True)

    @pl.when(jnp.logical_not(on_plane))
    def _():
        sequence(9, False)


    def both_halves(ref, base, tile):
        def half(at):
            off = lax.rem(at - z + NZ, NZ)
            return ref[base + jnp.where(off <= 4, jnp.maximum(2 * off - 1, 0), 2 * (NZ - off))]

        return jnp.concatenate([half(2 * tile), half(2 * tile + 1)], 0)

    def factors(a, b, far):
        a = jnp.clip(a, 0, 3)
        b = jnp.clip(b, 0, 15)
        return product(both_halves(rows_ref, 8 * far, a), both_halves(cols_ref, (b % 4) * 8, b // 4))

    def renew(raw, first, count, parts):
        for u in range(count):
            value = raw(u).astype(jnp.float32) - parts[u]
            pool[first + u] = value.astype(jnp.bfloat16)

    @pl.loop(0, 5)
    def _(q):
        parts = [factors(map_ref[0, q * 8 + u], map_ref[1, q * 8 + u], 0) for u in range(8)]
        renew(lambda u: pool[q * 8 + u], q * 8, 8, parts)

    partner_info.wait()
    place_info = local(info_ref, info_at, 2)
    place_info.start()
    place_info.wait()
    for item in exchange:
        item.wait()
    parts = [factors(info_at[u, 0], info_at[u, 1], 1) for u in range(6)]
    renew(lambda u: recv_buf[u], 40, 6, parts)
    for h in range(4):
        for item in own_hop(h) + part_hop(h):
            item.wait_send()
    partner_piece.wait_send()


def place_kernel(place_ref, pool_ref, factor_in, factor_out, out_ref, zeros, sem, factor_sem):
    held = out_ref.shape[0]
    factor_copy = pltpu.make_async_copy(factor_in, factor_out, factor_sem)
    factor_copy.start()
    zeros[...] = jnp.zeros_like(zeros)

    @pl.loop(0, held)
    def _(j):
        s = place_ref[j]

        @pl.when(s >= 0)
        def _():
            pltpu.make_async_copy(pool_ref.at[jnp.clip(s, 0, 45)], out_ref.at[j], sem.at[j]).start()

        @pl.when(s < 0)
        def _():
            pltpu.make_async_copy(zeros, out_ref.at[j], sem.at[j]).start()

    @pl.loop(0, held)
    def _(j):
        pltpu.make_async_copy(zeros, out_ref.at[j], sem.at[j]).wait()

    factor_copy.wait()


def shards(panel, diag_inverse, tiles, tile_map, send_list, place_list):
    vmem = pl.BlockSpec(memory_space=pltpu.VMEM)
    smem = pl.BlockSpec(memory_space=pltpu.SMEM)
    hbm = pl.BlockSpec(memory_space=pltpu.HBM)
    bf16 = jnp.bfloat16
    held = place_list.shape[0]
    factor, pool = pl.pallas_call(
        panel_kernel,
        out_shape=(
            pltpu.VMEM((128, 256), jnp.float32),
            pltpu.VMEM((46, 256, 256), bf16),
        ),
        in_specs=[hbm] * 5,
        out_specs=(vmem, vmem),
        scratch_shapes=[
            pltpu.VMEM((128, 256), jnp.float32),
            pltpu.VMEM((256, 256), jnp.float32),
            pltpu.SMEM((2, 40), jnp.int32),
            pltpu.SMEM((6,), jnp.int32),
            pltpu.VMEM((16, 128, 256), bf16),
            pltpu.VMEM((32, 128, 256), bf16),
            pltpu.VMEM((6, 256, 256), bf16),
            pltpu.VMEM((6, 256, 256), bf16),
            pltpu.VMEM((8, 128), jnp.int32),
            pltpu.VMEM((8, 128), jnp.int32),
            pltpu.SMEM((8, 128), jnp.int32),
            pltpu.SemaphoreType.DMA((SEND.count,)),
            pltpu.SemaphoreType.DMA((RECV.count,)),
            pltpu.SemaphoreType.DMA((5,)),
        ],
        compiler_params=pltpu.CompilerParams(
            collective_id=0, has_side_effects=True, vmem_limit_bytes=54 * 1024 * 1024
        ),
        name="gather_exchange_renew",
    )(panel, diag_inverse, tiles, tile_map.T, send_list)
    return pl.pallas_call(
        place_kernel,
        out_shape=(
            jax.ShapeDtypeStruct((128, 256), jnp.float32),
            jax.ShapeDtypeStruct((held, 256, 256), bf16),
        ),
        in_specs=[smem, pl.BlockSpec(memory_space=pl.ANY), pl.BlockSpec(memory_space=pl.ANY)],
        out_specs=(hbm, hbm),
        scratch_shapes=[
            pltpu.VMEM((256, 256), bf16),
            pltpu.SemaphoreType.DMA((held,)),
            pltpu.SemaphoreType.DMA,
        ],
        compiler_params=pltpu.CompilerParams(vmem_limit_bytes=4 * 1024 * 1024),
        name="place",
    )(place_list, pool, factor)


def solution(mesh):
    in_specs = (
        P(("row", "col"), None),
        P(),
        P(("row", "col"), None, None),
        P(("row", "col"), None),
        P(("row", "col")),
        P(("row", "col")),
    )
    out_specs = (P(("row", "col"), None), P(("row", "col"), None, None))
    return jax.shard_map(shards, mesh=mesh, in_specs=in_specs, out_specs=out_specs, check_vma=False)
```

```python
import functools

import jax
import jax.numpy as jnp
from jax import lax
from jax.experimental import pallas as pl
from jax.experimental.pallas import tpu as pltpu
from jax.sharding import PartitionSpec as P

MESH = pl.DeviceIdType.MESH
NX, NY, NZ = 4, 4, 8
PLACE = {0: 0, 1: 1, -1: 2, 2: 3, -2: 4, 3: 5, -3: 6, 4: 7, -4: 7}
HOPS = ((0, 1), (1, 2), (3, 2), (5, 2), (7, 1))
PARTNER_TICK = 2
EXCHANGE_TICK = (0, 1, 2, 4, 6, 8)


class Ids:
    def __init__(self):
        self.count = 0

    def take(self, n):
        first = self.count
        self.count += n
        return first


SEND, RECV = Ids(), Ids()
S_ZP, S_ZM, S_QP, S_QM = (SEND.take(4) for _ in range(4))
S_PP, S_INFO = SEND.take(1), SEND.take(1)
S_EX = SEND.take(6)
S_YI, S_YC, S_YO, S_XC, S_XI, S_XF = (SEND.take(5) for _ in range(6))
S_DD = SEND.take(20)
R_ZP, R_ZM, R_QP, R_QM = (RECV.take(4) for _ in range(4))
R_PP, R_INFO = RECV.take(1), RECV.take(1)
R_EX = RECV.take(6)
R_AY, R_RC, R_RI, R_RF = (RECV.take(5) for _ in range(4))
R_DD = RECV.take(20)


def solve(panel, inverse):
    return lax.dot_general(
        panel,
        inverse,
        (((1,), (1,)), ((), ())),
        precision=lax.Precision.HIGHEST,
        preferred_element_type=jnp.float32,
    )


def product(left, right):
    return lax.dot_general(
        left, right, (((1,), (1,)), ((), ())), preferred_element_type=jnp.float32
    )


def panel_kernel(
    panel_hbm, inv_hbm, tiles_hbm, map_hbm, send_hbm,
    factor_ref, pool,
    panel_ref, inv_ref, map_ref, send_ref, rows_ref, cols_ref,
    send_buf, recv_buf, info_src, info_ref, info_at, send_sem, recv_sem, local_sem,
):
    r = lax.axis_index("row")
    z = lax.axis_index("col")
    x, y, k = r // 8, (r // 2) % 4, r % 2

    def dev(px, py, pk, pz):
        return (px * 8 + py * 2 + pk, pz)

    xi, xc = x + 1 - 2 * (x % 2), 3 - x
    yi, yc = y + 1 - 2 * (y % 2), 3 - y
    d_zp, d_zm = dev(x, y, k, (z + 1) % NZ), dev(x, y, k, (z + NZ - 1) % NZ)
    d_part = dev(3 - x, 3 - y, 1 - k, z)
    d_xi, d_xc = dev(xi, y, k, z), dev(xc, y, k, z)
    d_yi, d_yc = dev(x, yi, k, z), dev(x, yc, k, z)
    d_core = dev(x, y, 1 - k, z)
    full = (r >= 24) & (r - 24 >= z)
    far_r = 31 - r
    partner_full = (far_r >= 24) & (far_r - 24 >= z)
    d_xo = dev(3 - xi, y, k, z)
    d_far = dev(x, 3 - yi, k, z)
    sy, sk = z // 2, z % 2

    barrier = pltpu.get_barrier_semaphore()
    friends = (d_zp, d_zm, d_part, d_xi, d_xc, d_yi, d_yc, d_far, d_xo, d_core)
    for friend in friends:
        pl.semaphore_signal(barrier, inc=1, device_id=friend, device_id_type=MESH)

    def local(src, dst, i):
        return pltpu.make_async_copy(src, dst, local_sem.at[i])

    load_panel = local(panel_hbm, panel_ref, 0)
    load_inv = local(inv_hbm, inv_ref, 1)
    load_map = local(map_hbm, map_ref, 2)
    load_send = local(send_hbm, send_ref, 3)
    load_tiles = local(tiles_hbm, pool.at[pl.ds(0, 40)], 4)
    for item in (load_panel, load_inv, load_map, load_send, load_tiles):
        item.start()
    load_panel.wait()
    load_inv.wait()
    factor = solve(panel_ref[...], inv_ref[...])
    factor_ref[...] = factor
    rows_ref[0] = factor.astype(jnp.bfloat16)

    def copy(src, dst, s, t, device):
        return pltpu.make_async_remote_copy(
            src_ref=src, dst_ref=dst, send_sem=send_sem.at[s], recv_sem=recv_sem.at[t],
            device_id=device, device_id_type=MESH,
        )

    def ring(base, h, up, s0, t0):
        sign = -1 if up else 1
        src, dst = base + PLACE[sign * h], base + PLACE[sign * (h + 1)]
        device = d_zp if up else d_zm
        if h < 3:
            return copy(rows_ref.at[src], rows_ref.at[dst], s0 + h, t0 + h, device)
        part = pl.ds(0, 64) if up else pl.ds(64, 64)
        return copy(rows_ref.at[src, part], rows_ref.at[dst, part], s0 + h, t0 + h, device)

    def ring_wait_recv(base, h, r_up, r_down):
        for sign, t, part in ((-1, r_up, pl.ds(0, 64)), (1, r_down, pl.ds(64, 64))):
            at = rows_ref.at[base + PLACE[sign * h]]
            if h == 4:
                at = rows_ref.at[base + PLACE[4], part]
            copy(at, at, 0, t + h - 1, d_zp).wait_recv()

    def own_hop(h):
        return (ring(0, h, True, S_ZP, R_ZP), ring(0, h, False, S_ZM, R_ZM))

    def part_hop(h):
        return (ring(8, h, True, S_QP, R_QP), ring(8, h, False, S_QM, R_QM))

    def start(copies):
        for item in copies:
            item.start()

    partner_piece = copy(rows_ref.at[0], rows_ref.at[8], S_PP, R_PP, d_part)
    partner_info = copy(info_src, info_ref, S_INFO, R_INFO, d_part)
    exchange = [
        copy(send_buf.at[j], recv_buf.at[j], S_EX + j, R_EX + j, d_part) for j in range(6)
    ]

    def cols_at(block, g):
        return cols_ref.at[pl.ds(block * 8 + HOPS[g][0], HOPS[g][1])]

    def mine(g, source):
        return rows_ref.at[pl.ds(*HOPS[g])] if source else cols_at(x, g)

    def y_in(g, source):
        return copy(mine(g, source), cols_at(x, g), S_YI + g, R_AY + g, d_yi)

    def y_cross(g, source):
        return copy(mine(g, source), cols_at(x, g), S_YC + g, R_AY + g, d_yc)

    def y_over(g):
        return copy(mine(g, True), cols_at(x, g), S_YO + g, R_AY + g, d_far)

    def x_cross(g, source):
        return copy(mine(g, source), cols_at(x, g), S_XC + g, R_RC + g, d_xc)

    def x_in(g, source):
        return copy(mine(g, source), cols_at(x, g), S_XI + g, R_RI + g, d_xi)

    def x_over(g, source):
        return copy(mine(g, source), cols_at(x, g), S_XF + g, R_RF + g, d_xo)

    def to_core(which, g, source):
        block = (x, xc, xi, 3 - xi)[which]
        src = mine(g, source) if which == 0 else cols_at(block, g)
        return copy(src, cols_at(block, g), S_DD + which * 5 + g, R_DD + which * 5 + g, d_core)

    def arrived(ref, t):
        copy(ref, ref, 0, t, d_core).wait_recv()

    pl.semaphore_wait(barrier, len(friends))
    start(own_hop(0))
    partner_piece.start()
    load_map.wait()
    load_send.wait()
    load_tiles.wait()
    lane = lax.broadcasted_iota(jnp.int32, (8, 128), 1)
    sub = lax.broadcasted_iota(jnp.int32, (8, 128), 0)
    info = jnp.zeros((8, 128), jnp.int32)
    for j in range(6):
        slot = jnp.clip(send_ref[j], 0, 39)
        send_buf[j] = pool[slot]
        info = jnp.where((sub == j) & (lane == 0), map_ref[0, slot], info)
        info = jnp.where((sub == j) & (lane == 1), map_ref[1, slot], info)
    info_src[...] = info
    partner_info.start()


    def sequence(depth, plane):
        source = depth == 0
        for t in range(0, 10):
            for j in range(6):
                if EXCHANGE_TICK[j] == t:
                    pl.when(jnp.logical_not(partner_full))(exchange[j].start)
            if 1 <= t <= 4:
                ring_wait_recv(0, t, R_ZP, R_ZM)
                if t <= 3:
                    start(own_hop(t))
            p = t - PARTNER_TICK
            if p == 0:
                partner_piece.wait_recv()
                start(part_hop(0))
            elif 1 <= p <= 4:
                ring_wait_recv(8, p, R_QP, R_QM)
                if p <= 3:
                    start(part_hop(p))
            if not plane:
                continue
            g = t - depth
            if 0 <= g <= 4:
                if source:
                    y_cross(g, source).start()
                    y_over(g).start()
                    y_in(g, source).start()
                else:
                    arrived(cols_at(x, g), R_AY + g)
                x_cross(g, source).start()
                x_over(g, source).start()
                x_in(g, source).start()
                to_core(0, g, source).start()
            g = t - depth - 2
            if 0 <= g <= 4:
                arrived(cols_at(xc, g), R_RC + g)
                to_core(1, g, source).start()
                arrived(cols_at(xi, g), R_RI + g)
                to_core(2, g, source).start()
            g = t - depth - 2
            if 0 <= g <= 4:
                arrived(cols_at(3 - xi, g), R_RF + g)
                to_core(3, g, source).start()
        if source:
            for i in range(8):
                cols_ref[x * 8 + i] = rows_ref[i]
        if plane:
            for g in range(5):
                if source:
                    y_in(g, source).wait_send()
                    y_over(g).wait_send()
                    y_cross(g, source).wait_send()
                x_cross(g, source).wait_send()
                x_in(g, source).wait_send()
                x_over(g, source).wait_send()
            for which in range(4):
                for g in range(5):
                    to_core(which, g, source).wait_send()
        else:
            for which in range(4):
                for g in range(5):
                    to_core(which, g, False).wait_recv()

    on_plane = k == sk
    is_source = y == sy
    is_far = y == (3 - sy) + 1 - 2 * ((3 - sy) % 2)

    @pl.when(on_plane & is_source)
    def _():
        sequence(0, True)

    @pl.when(on_plane & jnp.logical_not(is_source) & jnp.logical_not(is_far))
    def _():
        sequence(1, True)

    @pl.when(on_plane & is_far)
    def _():
        sequence(1, True)

    @pl.when(jnp.logical_not(on_plane))
    def _():
        sequence(9, False)


    def both_halves(ref, base, tile):
        def half(at):
            off = lax.rem(at - z + NZ, NZ)
            return ref[base + jnp.where(off <= 4, jnp.maximum(2 * off - 1, 0), 2 * (NZ - off))]

        return jnp.concatenate([half(2 * tile), half(2 * tile + 1)], 0)

    def factors(a, b, far):
        a = jnp.clip(a, 0, 3)
        b = jnp.clip(b, 0, 15)
        return product(both_halves(rows_ref, 8 * far, a), both_halves(cols_ref, (b % 4) * 8, b // 4))

    def renew(raw, first, count, parts):
        for u in range(count):
            value = raw(u).astype(jnp.float32) - parts[u]
            pool[first + u] = value.astype(jnp.bfloat16)

    @pl.loop(0, 5)
    def _(q):
        parts = [factors(map_ref[0, q * 8 + u], map_ref[1, q * 8 + u], 0) for u in range(8)]
        renew(lambda u: pool[q * 8 + u], q * 8, 8, parts)

    partner_info.wait()
    place_info = local(info_ref, info_at, 2)
    place_info.start()
    place_info.wait()
    @pl.when(jnp.logical_not(full))
    def _():
        for item in exchange:
            item.wait_recv()
        parts = [factors(info_at[u, 0], info_at[u, 1], 1) for u in range(6)]
        renew(lambda u: recv_buf[u], 40, 6, parts)

    @pl.when(jnp.logical_not(partner_full))
    def _():
        for item in exchange:
            item.wait_send()

    for h in range(4):
        for item in own_hop(h) + part_hop(h):
            item.wait_send()
    partner_piece.wait_send()


def place_kernel(place_ref, pool_ref, factor_in, factor_out, out_ref, zeros, sem, factor_sem):
    held = out_ref.shape[0]
    factor_copy = pltpu.make_async_copy(factor_in, factor_out, factor_sem)
    factor_copy.start()
    zeros[...] = jnp.zeros_like(zeros)

    @pl.loop(0, held)
    def _(j):
        s = place_ref[j]

        @pl.when(s >= 0)
        def _():
            pltpu.make_async_copy(pool_ref.at[jnp.clip(s, 0, 45)], out_ref.at[j], sem.at[j]).start()

        @pl.when(s < 0)
        def _():
            pltpu.make_async_copy(zeros, out_ref.at[j], sem.at[j]).start()

    @pl.loop(0, held)
    def _(j):
        pltpu.make_async_copy(zeros, out_ref.at[j], sem.at[j]).wait()

    factor_copy.wait()


def shards(panel, diag_inverse, tiles, tile_map, send_list, place_list):
    vmem = pl.BlockSpec(memory_space=pltpu.VMEM)
    smem = pl.BlockSpec(memory_space=pltpu.SMEM)
    hbm = pl.BlockSpec(memory_space=pltpu.HBM)
    bf16 = jnp.bfloat16
    held = place_list.shape[0]
    factor, pool = pl.pallas_call(
        panel_kernel,
        out_shape=(
            pltpu.VMEM((128, 256), jnp.float32),
            pltpu.VMEM((46, 256, 256), bf16),
        ),
        in_specs=[hbm] * 5,
        out_specs=(vmem, vmem),
        scratch_shapes=[
            pltpu.VMEM((128, 256), jnp.float32),
            pltpu.VMEM((256, 256), jnp.float32),
            pltpu.SMEM((2, 40), jnp.int32),
            pltpu.SMEM((6,), jnp.int32),
            pltpu.VMEM((16, 128, 256), bf16),
            pltpu.VMEM((32, 128, 256), bf16),
            pltpu.VMEM((6, 256, 256), bf16),
            pltpu.VMEM((6, 256, 256), bf16),
            pltpu.VMEM((8, 128), jnp.int32),
            pltpu.VMEM((8, 128), jnp.int32),
            pltpu.SMEM((8, 128), jnp.int32),
            pltpu.SemaphoreType.DMA((SEND.count,)),
            pltpu.SemaphoreType.DMA((RECV.count,)),
            pltpu.SemaphoreType.DMA((5,)),
        ],
        compiler_params=pltpu.CompilerParams(
            collective_id=0, has_side_effects=True, vmem_limit_bytes=54 * 1024 * 1024
        ),
        name="gather_exchange_renew",
    )(panel, diag_inverse, tiles, tile_map.T, send_list)
    return pl.pallas_call(
        place_kernel,
        out_shape=(
            jax.ShapeDtypeStruct((128, 256), jnp.float32),
            jax.ShapeDtypeStruct((held, 256, 256), bf16),
        ),
        in_specs=[smem, pl.BlockSpec(memory_space=pl.ANY), pl.BlockSpec(memory_space=pl.ANY)],
        out_specs=(hbm, hbm),
        scratch_shapes=[
            pltpu.VMEM((256, 256), bf16),
            pltpu.SemaphoreType.DMA((held,)),
            pltpu.SemaphoreType.DMA,
        ],
        compiler_params=pltpu.CompilerParams(vmem_limit_bytes=4 * 1024 * 1024),
        name="place",
    )(place_list, pool, factor)


def solution(mesh):
    in_specs = (
        P(("row", "col"), None),
        P(),
        P(("row", "col"), None, None),
        P(("row", "col"), None),
        P(("row", "col")),
        P(("row", "col")),
    )
    out_specs = (P(("row", "col"), None), P(("row", "col"), None, None))
    return jax.shard_map(shards, mesh=mesh, in_specs=in_specs, out_specs=out_specs, check_vma=False)
```

```python
import functools

import jax
import jax.numpy as jnp
from jax import lax
from jax.experimental import pallas as pl
from jax.experimental.pallas import tpu as pltpu
from jax.sharding import PartitionSpec as P

MESH = pl.DeviceIdType.MESH
NX, NY, NZ = 4, 4, 8
PLACE = {0: 0, 1: 1, -1: 2, 2: 3, -2: 4, 3: 5, -3: 6, 4: 7, -4: 7}
HOPS = ((0, 1), (1, 2), (3, 2), (5, 2), (7, 1))
PARTNER_TICK = 2
EXCHANGE_TICK = (0, 1, 2, 4, 5, 7)


class Ids:
    def __init__(self):
        self.count = 0

    def take(self, n):
        first = self.count
        self.count += n
        return first


SEND, RECV = Ids(), Ids()
S_ZP, S_ZM, S_QP, S_QM = (SEND.take(4) for _ in range(4))
S_PP, S_INFO = SEND.take(1), SEND.take(1)
S_EX = SEND.take(6)
S_YI, S_YC, S_YO, S_XC, S_XI, S_XF = (SEND.take(5) for _ in range(6))
S_DD = SEND.take(20)
R_ZP, R_ZM, R_QP, R_QM = (RECV.take(4) for _ in range(4))
R_PP, R_INFO = RECV.take(1), RECV.take(1)
R_EX = RECV.take(6)
R_AY, R_RC, R_RI, R_RF = (RECV.take(5) for _ in range(4))
R_DD = RECV.take(20)


def solve(panel, inverse):
    return lax.dot_general(
        panel,
        inverse,
        (((1,), (1,)), ((), ())),
        precision=lax.Precision.HIGHEST,
        preferred_element_type=jnp.float32,
    )


def product(left, right):
    return lax.dot_general(
        left, right, (((1,), (1,)), ((), ())), preferred_element_type=jnp.float32
    )


def panel_kernel(
    panel_hbm, inv_hbm, tiles_hbm, map_hbm, send_hbm,
    factor_ref, pool,
    panel_ref, inv_ref, map_ref, send_ref, rows_ref, cols_ref,
    send_buf, recv_buf, info_src, info_ref, info_at, send_sem, recv_sem, local_sem,
):
    r = lax.axis_index("row")
    z = lax.axis_index("col")
    x, y, k = r // 8, (r // 2) % 4, r % 2

    def dev(px, py, pk, pz):
        return (px * 8 + py * 2 + pk, pz)

    xi, xc = x + 1 - 2 * (x % 2), 3 - x
    yi, yc = y + 1 - 2 * (y % 2), 3 - y
    d_zp, d_zm = dev(x, y, k, (z + 1) % NZ), dev(x, y, k, (z + NZ - 1) % NZ)
    d_part = dev(3 - x, 3 - y, 1 - k, z)
    d_xi, d_xc = dev(xi, y, k, z), dev(xc, y, k, z)
    d_yi, d_yc = dev(x, yi, k, z), dev(x, yc, k, z)
    d_core = dev(x, y, 1 - k, z)
    full = (r >= 24) & (r - 24 >= z)
    far_r = 31 - r
    partner_full = (far_r >= 24) & (far_r - 24 >= z)
    d_xo = dev(3 - xi, y, k, z)
    d_far = dev(x, 3 - yi, k, z)
    sy, sk = z // 2, z % 2

    barrier = pltpu.get_barrier_semaphore()
    friends = (d_zp, d_zm, d_part, d_xi, d_xc, d_yi, d_yc, d_far, d_xo, d_core)
    for friend in friends:
        pl.semaphore_signal(barrier, inc=1, device_id=friend, device_id_type=MESH)

    def local(src, dst, i):
        return pltpu.make_async_copy(src, dst, local_sem.at[i])

    load_panel = local(panel_hbm, panel_ref, 0)
    load_inv = local(inv_hbm, inv_ref, 1)
    load_map = local(map_hbm, map_ref, 2)
    load_send = local(send_hbm, send_ref, 3)
    load_tiles = local(tiles_hbm, pool.at[pl.ds(0, 40)], 4)
    for item in (load_panel, load_inv, load_map, load_send, load_tiles):
        item.start()
    load_panel.wait()
    load_inv.wait()
    factor = solve(panel_ref[...], inv_ref[...])
    factor_ref[...] = factor
    rows_ref[0] = factor.astype(jnp.bfloat16)

    def copy(src, dst, s, t, device):
        return pltpu.make_async_remote_copy(
            src_ref=src, dst_ref=dst, send_sem=send_sem.at[s], recv_sem=recv_sem.at[t],
            device_id=device, device_id_type=MESH,
        )

    def ring(base, h, up, s0, t0):
        sign = -1 if up else 1
        src, dst = base + PLACE[sign * h], base + PLACE[sign * (h + 1)]
        device = d_zp if up else d_zm
        if h < 3:
            return copy(rows_ref.at[src], rows_ref.at[dst], s0 + h, t0 + h, device)
        part = pl.ds(0, 64) if up else pl.ds(64, 64)
        return copy(rows_ref.at[src, part], rows_ref.at[dst, part], s0 + h, t0 + h, device)

    def ring_wait_recv(base, h, r_up, r_down):
        for sign, t, part in ((-1, r_up, pl.ds(0, 64)), (1, r_down, pl.ds(64, 64))):
            at = rows_ref.at[base + PLACE[sign * h]]
            if h == 4:
                at = rows_ref.at[base + PLACE[4], part]
            copy(at, at, 0, t + h - 1, d_zp).wait_recv()

    def own_hop(h):
        return (ring(0, h, True, S_ZP, R_ZP), ring(0, h, False, S_ZM, R_ZM))

    def part_hop(h):
        return (ring(8, h, True, S_QP, R_QP), ring(8, h, False, S_QM, R_QM))

    def start(copies):
        for item in copies:
            item.start()

    partner_piece = copy(rows_ref.at[0], rows_ref.at[8], S_PP, R_PP, d_part)
    partner_info = copy(info_src, info_ref, S_INFO, R_INFO, d_part)
    exchange = [
        copy(send_buf.at[j], recv_buf.at[j], S_EX + j, R_EX + j, d_part) for j in range(6)
    ]

    def cols_at(block, g):
        return cols_ref.at[pl.ds(block * 8 + HOPS[g][0], HOPS[g][1])]

    def mine(g, source):
        return rows_ref.at[pl.ds(*HOPS[g])] if source else cols_at(x, g)

    def y_in(g, source):
        return copy(mine(g, source), cols_at(x, g), S_YI + g, R_AY + g, d_yi)

    def y_cross(g, source):
        return copy(mine(g, source), cols_at(x, g), S_YC + g, R_AY + g, d_yc)

    def y_over(g):
        return copy(mine(g, True), cols_at(x, g), S_YO + g, R_AY + g, d_far)

    def x_cross(g, source):
        return copy(mine(g, source), cols_at(x, g), S_XC + g, R_RC + g, d_xc)

    def x_in(g, source):
        return copy(mine(g, source), cols_at(x, g), S_XI + g, R_RI + g, d_xi)

    def x_over(g, source):
        return copy(mine(g, source), cols_at(x, g), S_XF + g, R_RF + g, d_xo)

    def to_core(which, g, source):
        block = (x, xc, xi, 3 - xi)[which]
        src = mine(g, source) if which == 0 else cols_at(block, g)
        return copy(src, cols_at(block, g), S_DD + which * 5 + g, R_DD + which * 5 + g, d_core)

    def arrived(ref, t):
        copy(ref, ref, 0, t, d_core).wait_recv()

    pl.semaphore_wait(barrier, len(friends))
    start(own_hop(0))
    partner_piece.start()
    load_map.wait()
    load_send.wait()
    load_tiles.wait()
    lane = lax.broadcasted_iota(jnp.int32, (8, 128), 1)
    sub = lax.broadcasted_iota(jnp.int32, (8, 128), 0)
    info = jnp.zeros((8, 128), jnp.int32)
    for j in range(6):
        slot = jnp.clip(send_ref[j], 0, 39)
        send_buf[j] = pool[slot]
        info = jnp.where((sub == j) & (lane == 0), map_ref[0, slot], info)
        info = jnp.where((sub == j) & (lane == 1), map_ref[1, slot], info)
    info_src[...] = info
    partner_info.start()


    def sequence(depth, plane):
        source = depth == 0
        for t in range(0, 10):
            for j in range(6):
                if EXCHANGE_TICK[j] == t:
                    pl.when(jnp.logical_not(partner_full))(exchange[j].start)
            if 1 <= t <= 4:
                ring_wait_recv(0, t, R_ZP, R_ZM)
                if t <= 3:
                    start(own_hop(t))
            p = t - PARTNER_TICK
            if p == 0:
                partner_piece.wait_recv()
                start(part_hop(0))
            elif 1 <= p <= 4:
                ring_wait_recv(8, p, R_QP, R_QM)
                if p <= 3:
                    start(part_hop(p))
            if not plane:
                continue
            g = t - depth
            if 0 <= g <= 4:
                if source:
                    y_cross(g, source).start()
                    y_over(g).start()
                    y_in(g, source).start()
                else:
                    arrived(cols_at(x, g), R_AY + g)
                x_cross(g, source).start()
                x_over(g, source).start()
                x_in(g, source).start()
                to_core(0, g, source).start()
            g = t - depth - 2
            if 0 <= g <= 4:
                arrived(cols_at(xc, g), R_RC + g)
                to_core(1, g, source).start()
                arrived(cols_at(xi, g), R_RI + g)
                to_core(2, g, source).start()
            g = t - depth - 2
            if 0 <= g <= 4:
                arrived(cols_at(3 - xi, g), R_RF + g)
                to_core(3, g, source).start()
        if source:
            for i in range(8):
                cols_ref[x * 8 + i] = rows_ref[i]
        if plane:
            for g in range(5):
                if source:
                    y_in(g, source).wait_send()
                    y_over(g).wait_send()
                    y_cross(g, source).wait_send()
                x_cross(g, source).wait_send()
                x_in(g, source).wait_send()
                x_over(g, source).wait_send()
            for which in range(4):
                for g in range(5):
                    to_core(which, g, source).wait_send()
        else:
            for which in range(4):
                for g in range(5):
                    to_core(which, g, False).wait_recv()

    on_plane = k == sk
    is_source = y == sy
    is_far = y == (3 - sy) + 1 - 2 * ((3 - sy) % 2)

    @pl.when(on_plane & is_source)
    def _():
        sequence(0, True)

    @pl.when(on_plane & jnp.logical_not(is_source) & jnp.logical_not(is_far))
    def _():
        sequence(1, True)

    @pl.when(on_plane & is_far)
    def _():
        sequence(1, True)

    @pl.when(jnp.logical_not(on_plane))
    def _():
        sequence(9, False)


    def both_halves(ref, base, tile):
        def half(at):
            off = lax.rem(at - z + NZ, NZ)
            return ref[base + jnp.where(off <= 4, jnp.maximum(2 * off - 1, 0), 2 * (NZ - off))]

        return jnp.concatenate([half(2 * tile), half(2 * tile + 1)], 0)

    def factors(a, b, far):
        a = jnp.clip(a, 0, 3)
        b = jnp.clip(b, 0, 15)
        return product(both_halves(rows_ref, 8 * far, a), both_halves(cols_ref, (b % 4) * 8, b // 4))

    def renew(raw, first, count, parts):
        for u in range(count):
            value = raw(u).astype(jnp.float32) - parts[u]
            pool[first + u] = value.astype(jnp.bfloat16)

    @pl.loop(0, 5)
    def _(q):
        parts = [factors(map_ref[0, q * 8 + u], map_ref[1, q * 8 + u], 0) for u in range(8)]
        renew(lambda u: pool[q * 8 + u], q * 8, 8, parts)

    partner_info.wait()
    place_info = local(info_ref, info_at, 2)
    place_info.start()
    place_info.wait()
    @pl.when(jnp.logical_not(full))
    def _():
        for item in exchange:
            item.wait_recv()
        parts = [factors(info_at[u, 0], info_at[u, 1], 1) for u in range(6)]
        renew(lambda u: recv_buf[u], 40, 6, parts)

    @pl.when(jnp.logical_not(partner_full))
    def _():
        for item in exchange:
            item.wait_send()

    for h in range(4):
        for item in own_hop(h) + part_hop(h):
            item.wait_send()
    partner_piece.wait_send()


def place_kernel(place_ref, pool_ref, factor_in, factor_out, out_ref, zeros, sem, factor_sem):
    held = out_ref.shape[0]
    factor_copy = pltpu.make_async_copy(factor_in, factor_out, factor_sem)
    factor_copy.start()
    zeros[...] = jnp.zeros_like(zeros)

    @pl.loop(0, held)
    def _(j):
        s = place_ref[j]

        @pl.when(s >= 0)
        def _():
            pltpu.make_async_copy(pool_ref.at[jnp.clip(s, 0, 45)], out_ref.at[j], sem.at[j]).start()

        @pl.when(s < 0)
        def _():
            pltpu.make_async_copy(zeros, out_ref.at[j], sem.at[j]).start()

    @pl.loop(0, held)
    def _(j):
        pltpu.make_async_copy(zeros, out_ref.at[j], sem.at[j]).wait()

    factor_copy.wait()


def shards(panel, diag_inverse, tiles, tile_map, send_list, place_list):
    vmem = pl.BlockSpec(memory_space=pltpu.VMEM)
    smem = pl.BlockSpec(memory_space=pltpu.SMEM)
    hbm = pl.BlockSpec(memory_space=pltpu.HBM)
    bf16 = jnp.bfloat16
    held = place_list.shape[0]
    factor, pool = pl.pallas_call(
        panel_kernel,
        out_shape=(
            pltpu.VMEM((128, 256), jnp.float32),
            pltpu.VMEM((46, 256, 256), bf16),
        ),
        in_specs=[hbm] * 5,
        out_specs=(vmem, vmem),
        scratch_shapes=[
            pltpu.VMEM((128, 256), jnp.float32),
            pltpu.VMEM((256, 256), jnp.float32),
            pltpu.SMEM((2, 40), jnp.int32),
            pltpu.SMEM((6,), jnp.int32),
            pltpu.VMEM((16, 128, 256), bf16),
            pltpu.VMEM((32, 128, 256), bf16),
            pltpu.VMEM((6, 256, 256), bf16),
            pltpu.VMEM((6, 256, 256), bf16),
            pltpu.VMEM((8, 128), jnp.int32),
            pltpu.VMEM((8, 128), jnp.int32),
            pltpu.SMEM((8, 128), jnp.int32),
            pltpu.SemaphoreType.DMA((SEND.count,)),
            pltpu.SemaphoreType.DMA((RECV.count,)),
            pltpu.SemaphoreType.DMA((5,)),
        ],
        compiler_params=pltpu.CompilerParams(
            collective_id=0, has_side_effects=True, vmem_limit_bytes=54 * 1024 * 1024
        ),
        name="gather_exchange_renew",
    )(panel, diag_inverse, tiles, tile_map.T, send_list)
    return pl.pallas_call(
        place_kernel,
        out_shape=(
            jax.ShapeDtypeStruct((128, 256), jnp.float32),
            jax.ShapeDtypeStruct((held, 256, 256), bf16),
        ),
        in_specs=[smem, pl.BlockSpec(memory_space=pl.ANY), pl.BlockSpec(memory_space=pl.ANY)],
        out_specs=(hbm, hbm),
        scratch_shapes=[
            pltpu.VMEM((256, 256), bf16),
            pltpu.SemaphoreType.DMA((held,)),
            pltpu.SemaphoreType.DMA,
        ],
        compiler_params=pltpu.CompilerParams(vmem_limit_bytes=4 * 1024 * 1024),
        name="place",
    )(place_list, pool, factor)


def solution(mesh):
    in_specs = (
        P(("row", "col"), None),
        P(),
        P(("row", "col"), None, None),
        P(("row", "col"), None),
        P(("row", "col")),
        P(("row", "col")),
    )
    out_specs = (P(("row", "col"), None), P(("row", "col"), None, None))
    return jax.shard_map(shards, mesh=mesh, in_specs=in_specs, out_specs=out_specs, check_vma=False)
```
